32 devices in a mesh: pitch: 4 (over y, core), span: 8 (over z, x).
Axes of the slice: x: 2, y: 2, z: 4, core: 2. Of those that a mesh axis runs over, the one named last changes fastest.
Arguments:
- flow_state: float32 [4, 128, 512, 256], P(None, 'pitch', 'span'), may hold values from -6 to 6
- wall_inverse: float32 [64, 64], replicated, as said below
- metal_inverse: float32 [16, 16], replicated, as said below
- metal_state: float32 [16, 65536], P(None, ('pitch', 'span')), may hold values from -6 to 6
- metal_conduct: float32 [65536], P(('pitch', 'span')), may hold values from 0.3 to 3
- face_coef: float32 [2, 32768], P(None, ('pitch', 'span')), may hold values from 0.3 to 3
- owner_map: int32 [32768, 1], P(('pitch', 'span')), may hold values from 0 to 31; in each aligned block of 1024 rows (0 to 1023, 1024 to 2047, ...) at most 64 rows name the same one
- face_cell: int32 [32768], P(('pitch', 'span')), may hold values from 0 to 2047
- sample_col: int32 [32768], P(('pitch', 'span')), may hold values from 0 to 2047
- sample_low: int32 [32768], P(('pitch', 'span')), may hold values from 0 to 192
Outputs:
- new_state: float32 [4, 128, 512, 256], P(None, 'pitch', 'span')
- metal_out: float32 [16, 65536], P(None, ('pitch', 'span'))
The draws below stay inside these ranges and needn't reach their ends.
Inputs may be any that keep to these rules, and one draw needn't show every extreme that they name: `owner_map`: at most 64 faces of one device have the same owner; in every draw some device sends exactly 64 faces to one owner. `face_cell`: columns are numbered pitch cell times 64 plus span cell. `sample_col`: numbered as face_cell. `wall_inverse`: diagonal entries are the largest of their rows, within 0.5 to 1. `metal_inverse`: diagonal entries are the largest of their rows, within 0.5 to 1.
All inputs are finite; a program needn't handle non-finite values.
Results may differ from the reference program's by a relative error of at most 0.0001.
Values sent between devices are 32-bit elements; how exact they have to be, the bound alone decides.
A program may use at most 128 MiB of HBM per device.

```python
import math
import jax
import jax.numpy as jnp
import numpy as np
from jax import lax

CP = 32
CS = 64
GN = 256
F_DEV = 1024
WM = 64
MP = 16
PICARD = 3
CAP = 64
SLOT_DEV = 2048
SLOTS = 65536
F_TOTAL = 32768
NP = 128
NS = 512
N_SPAN = 8
DEVICES = 32


def inverse_table(key, order):
    key_diag = jax.random.fold_in(key, 11)
    key_off = jax.random.fold_in(key, 23)
    diagonal = jax.random.uniform(key_diag, (order,), jnp.float32, 0.5, 1.0)
    spread = 0.5 / order ** 0.5
    offdiag = jax.random.normal(key_off, (order, order), jnp.float32) * spread
    rows = jnp.arange(order)[:, None]
    cols = jnp.arange(order)[None, :]
    identity = (rows == cols).astype(jnp.float32)
    offdiag = jnp.clip(offdiag, -0.45, 0.45) * (1.0 - identity)
    return identity * diagonal[:, None] + offdiag


def draw_wall_inverse(key, part):
    return inverse_table(jax.random.fold_in(key, 101), WM)


def draw_metal_inverse(key, part):
    return inverse_table(jax.random.fold_in(key, 202), MP)


def place_ends(values, stream_key, low, high):
    index_at = [jax.random.randint(jax.random.fold_in(stream_key, axis), (), 0, length) for axis, length in enumerate(values.shape)]
    main_axis = values.shape.index(max(values.shape))
    next_to = index_at[:main_axis] + [(index_at[main_axis] + 1) % values.shape[main_axis]] + index_at[main_axis + 1:]
    return values.at[tuple(index_at)].set(low).at[tuple(next_to)].set(high)


def shard_levels(rng, dims, cuts, smallest, largest):
    def one(position, blocks):
        draws = jax.random.uniform(jax.random.fold_in(jax.random.fold_in(rng, 6), position), (blocks,), jnp.float32, smallest / len(cuts), largest / len(cuts))
        return jnp.repeat(jnp.exp(draws), dims[position] // blocks).reshape((-1,) + (1,) * (len(dims) - position - 1))

    gain = one(*cuts[0])
    for cut in cuts[1:]:
        gain = gain * one(*cut)
    return gain


def deal_out(rng, own, number, rows, count, top, reach, slope):
    ranking = jax.random.permutation(rng, count)
    heavy_load, common = portions_of(count, rows * top, reach, slope, True), portions_of(count, rows * top, reach, slope, False)
    places = jnp.arange(count)

    def named(lengths, turn):
        used = int((lengths > 0).sum())
        fixed = max(1, used // 4)
        shifted = fixed + (places - fixed + turn * (used - fixed)) % max(1, count - fixed)
        return jnp.zeros((count,), jnp.int32).at[ranking[jnp.where(places < fixed, places, shifted)]].set(jnp.asarray(lengths, jnp.int32))

    lengths = jnp.where(number % 4 == 0, named(heavy_load, number // 4), named(common, number - number // 4 - 1))
    mixed = jax.random.permutation(jax.random.fold_in(own, 3), count)
    source_of, sink = mixed[0:count // 2 * 2:2], mixed[1:count // 2 * 2:2]
    slack = jnp.minimum(lengths[source_of] - 1, reach - lengths[sink]) // 2
    slack = jnp.where((source_of == ranking[0]) | (sink == ranking[0]) | (lengths[sink] == 0), 0, jnp.maximum(slack, 0))
    shifted = jax.random.randint(jax.random.fold_in(own, 4), (count // 2,), 0, 1 << 20) % (slack + 1)
    lengths = lengths.at[source_of].add(-shifted).at[sink].add(shifted)
    labels = jnp.searchsorted(jnp.cumsum(lengths), jnp.arange(rows * top), side="right").astype(jnp.int32)
    listing = labels.reshape(top, rows).T
    listing = listing[jax.random.permutation(jax.random.fold_in(own, 1), rows)]
    turn = jax.random.randint(jax.random.fold_in(own, 2), (rows, 1), 0, top)
    return jnp.take_along_axis(listing, (jnp.arange(top)[None, :] + turn) % top, axis=1)


def portions_of(count, total, reach, skew, full):
    portions = [(1 << 20) // math.isqrt(standing ** skew) + 1 for standing in range(1, count + 1)]
    largest = reach if full else min(reach, max(-(-total // count), total * portions[0] // sum(portions)))
    least = 1 if total - largest >= count - 1 else 0
    given, spare = [largest] + [least] * (count - 1), total - largest - least * (count - 1)
    while spare > 0:
        movable = [i for i in range(1, count) if given[i] < largest] or [i for i in range(1, count) if given[i] < reach]
        pool, budget = sum([portions[i] for i in movable]), spare
        for i in movable:
            extra = min(reach - given[i], max(1, budget * portions[i] // pool), spare)
            given[i] = given[i] + extra
            spare = spare - extra
    return np.array(given)


def bell_draw(own_key, dims, scale, bound, cuts=(), kind=jnp.bfloat16):
    drawn = scale * jax.random.normal(own_key, dims, jnp.float32)
    if cuts:
        drawn = drawn * shard_levels(own_key, dims, cuts, -0.22, 0.18)
    return jnp.clip(drawn, -bound, bound).astype(kind)


def setup_inputs(seed: int = 0) -> dict:
    key_of = jax.random.split(jax.random.key(seed), 11)
    flow_state = bell_draw(key_of[0], (4, NP, NS, GN), 1.0, 6.0, ((1, 4), (2, 8)), jnp.float32)
    wall_inverse = draw_wall_inverse(jax.random.fold_in(key_of[10], 71), 0)
    metal_inverse = draw_metal_inverse(jax.random.fold_in(key_of[10], 71), 0)
    metal_state = bell_draw(key_of[3], (MP, SLOTS), 1.0, 6.0, ((1, 32),), jnp.float32)
    metal_conduct = jnp.clip(jnp.exp(math.log(3.0) - 2.3025851 * jax.random.uniform(key_of[4], (SLOTS,), jnp.float32) ** shard_levels(key_of[4], (SLOTS,), ((0, 32),), -0.2, 0.2)), 0.3, 3.0)
    face_coef = jnp.clip(jnp.exp(math.log(3.0) - 2.3025851 * jax.random.uniform(key_of[5], (2, F_TOTAL), jnp.float32) ** shard_levels(key_of[5], (2, F_TOTAL), ((1, 32),), -0.2, 0.2)), 0.3, 3.0)
    owner_map_keys = jax.random.split(jax.random.fold_in(key_of[6], 1), F_TOTAL // F_DEV)
    owner_map_turns = jax.random.permutation(jax.random.fold_in(key_of[6], 3), F_TOTAL // F_DEV)
    owner_map = jax.vmap(lambda own, number: deal_out(jax.random.fold_in(key_of[6], 2), own, number, F_DEV, DEVICES, 1, CAP, 1))(owner_map_keys, owner_map_turns).reshape((F_TOTAL, 1))
    face_cell = place_ends(jax.random.randint(key_of[7], (F_TOTAL,), 0, CP * CS), jax.random.fold_in(key_of[7], 1), 0, (CP * CS) - 1).astype(jnp.int32)
    sample_col = place_ends(jax.random.randint(key_of[8], (F_TOTAL,), 0, CP * CS), jax.random.fold_in(key_of[8], 1), 0, (CP * CS) - 1).astype(jnp.int32)
    sample_low = place_ends(jax.random.randint(key_of[9], (F_TOTAL,), 0, GN - WM + 1), jax.random.fold_in(key_of[9], 1), 0, GN - WM).astype(jnp.int32)
    return {"flow_state": flow_state, "wall_inverse": wall_inverse, "metal_inverse": metal_inverse, "metal_state": metal_state, "metal_conduct": metal_conduct, "face_coef": face_coef, "owner_map": owner_map, "face_cell": face_cell, "sample_col": sample_col, "sample_low": sample_low}


PRECISE = lax.Precision.HIGHEST
ALPHA_FLUID = 0.5
BETA_METAL = 0.5
DRAG_COEF = 0.5
TIME_STEP = 0.5
DIFFUSION = 0.2
ADVECTION = 0.6
WALL_AREA = 1.0

def wall_columns(packed, conduct_fluid, viscosity, metal_old, conduct_metal, occupied, wall_inverse, metal_inverse):
    slot_count = packed.shape[1]
    profiles = packed.reshape(3, WM, slot_count)
    force_u = profiles[0]
    force_w = profiles[1]
    force_t = profiles[2]
    speed_u = jnp.dot(wall_inverse, force_u, precision=PRECISE)
    speed_w = jnp.dot(wall_inverse, force_w, precision=PRECISE)
    for picard_step in range(PICARD):
        damping = DRAG_COEF / jnp.sqrt(1.0 + speed_u * speed_u + speed_w * speed_w)
        next_u = jnp.dot(wall_inverse, force_u - damping * speed_u, precision=PRECISE)
        next_w = jnp.dot(wall_inverse, force_w - damping * speed_w, precision=PRECISE)
        speed_u = next_u
        speed_w = next_w
    fluid_top = jnp.dot(wall_inverse[0], force_t, precision=PRECISE)
    metal_free = jnp.dot(metal_inverse, metal_old, precision=PRECISE)
    corner_fluid = wall_inverse[0, 0]
    corner_metal = metal_inverse[0, 0]
    denominator = conduct_fluid * (1.0 - ALPHA_FLUID * corner_fluid) + conduct_metal * (1.0 - BETA_METAL * corner_metal) + (1.0 - occupied)
    wall_temp = (conduct_fluid * fluid_top + conduct_metal * metal_free[0]) / denominator
    heat_flux = conduct_fluid * (fluid_top + (ALPHA_FLUID * corner_fluid - 1.0) * wall_temp)
    metal_new = metal_free + BETA_METAL * wall_temp[None, :] * metal_inverse[:, 0:1]
    fluxes = jnp.stack([viscosity * speed_u[0], viscosity * speed_w[0], heat_flux])
    return (fluxes, metal_new)

def advance(current, pitch_next, pitch_prev, span_next, span_prev, wall_source):
    normal_pad = jnp.pad(current, ((0, 0), (0, 0), (0, 0), (1, 1)), mode='edge')
    laplace = pitch_next + pitch_prev + span_next + span_prev + normal_pad[..., 2:] + normal_pad[..., :-2] - 6.0 * current
    tendency = DIFFUSION * laplace - ADVECTION * 0.5 * (pitch_next - pitch_prev)
    tendency = tendency.at[:3, :, :, 0].add(wall_source)
    return current + TIME_STEP * tendency

def reference(flow_state, wall_inverse, metal_inverse, metal_state, metal_conduct, face_coef, owner_map, face_cell, sample_col, sample_low):
    home_dev = jnp.arange(F_TOTAL, dtype=jnp.int32) // F_DEV
    target = owner_map[:, 0]
    choose = (target.reshape(DEVICES, F_DEV, 1) == jnp.arange(DEVICES, dtype=jnp.int32)[None, None, :]).astype(jnp.int32)
    before = lax.optimization_barrier(jnp.sum((jnp.cumsum(choose, axis=1) - choose) * choose, axis=2)).reshape(F_TOTAL)
    slot_global = target * SLOT_DEV + home_dev * CAP + before
    pitch_home = home_dev // N_SPAN
    span_home = home_dev % N_SPAN
    row_pitch = pitch_home * CP + sample_col // CS
    row_span = span_home * CS + sample_col % CS
    window = sample_low[:, None] + jnp.arange(WM, dtype=jnp.int32)[None, :]
    samples = flow_state[:3][:, row_pitch[:, None], row_span[:, None], window]
    packed = jnp.transpose(samples, (0, 2, 1)).reshape(3 * WM, F_TOTAL)
    occupied = jnp.ones((F_TOTAL,), jnp.float32)
    fluxes, metal_new = wall_columns(packed, face_coef[0], face_coef[1], metal_state[:, slot_global], metal_conduct[slot_global], occupied, wall_inverse, metal_inverse)
    metal_out = metal_state.at[:, slot_global].set(metal_new)
    cell_pitch = pitch_home * CP + face_cell // CS
    cell_span = span_home * CS + face_cell % CS
    column = cell_pitch * NS + cell_span
    summed = jax.ops.segment_sum(fluxes.T, column, num_segments=NP * NS)
    wall_source = -WALL_AREA * summed.T.reshape(3, NP, NS)
    pitch_next = jnp.roll(flow_state, -1, axis=1)
    pitch_prev = jnp.roll(flow_state, 1, axis=1)
    span_pad = jnp.pad(flow_state, ((0, 0), (0, 0), (1, 1), (0, 0)))
    new_state = advance(flow_state, pitch_next, pitch_prev, span_pad[:, :, 2:], span_pad[:, :, :-2], wall_source)
    return (new_state, metal_out)
```

```python
import functools
import jax
import jax.numpy as jnp
from jax import lax
from jax.experimental import pallas as pl
from jax.experimental.pallas import tpu as pltpu
from jax.sharding import PartitionSpec as P

PICARD = 3
ALPHA_FLUID = 0.5
BETA_METAL = 0.5
DRAG_COEF = 0.5
TIME_STEP = 0.5
DIFFUSION = 0.2
ADVECTION = 0.6
HALF = 64
LANES = 128
F32 = jnp.float32
BF16 = jnp.bfloat16
VMEM_LIMIT = 56 * 1024 * 1024
MESH = pl.DeviceIdType.MESH

NN = (((1,), (0,)), ((), ()))
NT = (((1,), (1,)), ((), ()))
TN = (((0,), (0,)), ((), ()))


def pieces(value, count):
    out = []
    for _ in range(count):
        part = value.astype(BF16)
        out.append(part)
        value = value - part.astype(F32)
    return out


def dot(a, b, dims):
    return lax.dot_general(a, b, dims, preferred_element_type=F32)


def dot3(a, b, dims):
    (a1, a2), (b1, b2) = (a, b)
    return dot(a1, b1, dims) + (dot(a1, b2, dims) + dot(a2, b1, dims))


def onehot(row, count, mask=None):
    index = lax.broadcasted_iota(jnp.int32, (count, row.shape[1]), 0)
    if mask is not None:
        index = index & mask
    return jnp.where(index == row, 1.0, 0.0).astype(F32)


def sample_kernel(
    devices,
    per_peer,
    span_cells,
    col_ref,
    metal_inv_ref,
    x_ref,
    low_ref,
    owner_ref,
    coef_ref,
    g_ref,
    metal_ref,
    conduct_ref,
    send_ref,
    faces_ref,
    edge_ref,
    xv,
    rows,
    gg,
    sem,
):
    comps = x_ref.shape[0]
    columns = x_ref.shape[1]
    pitch_cells = columns // span_cells
    faces = rows.shape[1]
    loads = [pltpu.make_async_copy(x_ref.at[c], xv.at[c], sem.at[c]) for c in range(comps)]
    for load in loads:
        load.start()
    gg[...] = jnp.zeros_like(gg)
    gg[0:HALF, 0:HALF] = g_ref[...]
    gg[HALF:LANES, HALF:LANES] = g_ref[...]
    table = pieces(gg[...], 2)
    row_pick = lax.broadcasted_iota(jnp.int32, (8, LANES), 0)
    lane_pick = lax.broadcasted_iota(jnp.int32, (8, LANES), 1)
    top_u = jnp.broadcast_to(gg[0:1, :], (8, LANES))
    top_w = jnp.broadcast_to(gg[HALF : HALF + 1, :], (8, LANES))
    top = pieces(jnp.where(row_pick == 0, top_u, jnp.where(row_pick == 1, top_w, 0.0)), 2)

    owner = owner_ref[...]
    choose = onehot(owner, devices)
    choose_b = choose.astype(BF16)
    up_row = lax.broadcasted_iota(jnp.int32, (LANES, LANES), 0)
    up_col = lax.broadcasted_iota(jnp.int32, (LANES, LANES), 1)
    upper = jnp.where(up_row < up_col, 1.0, 0.0).astype(BF16)
    running = jnp.zeros((devices, 1), F32)
    ranks = []
    for start in range(0, faces, LANES):
        block = choose[:, start : start + LANES]
        prior = dot(choose_b[:, start : start + LANES], upper, NN) + running
        ranks.append(jnp.sum(prior * block, axis=0, keepdims=True))
        running = running + jnp.sum(block, axis=1, keepdims=True)
    rank = jnp.concatenate(ranks, axis=1)

    free_top = jnp.zeros(metal_ref.shape[1:], F32)
    for i in range(metal_ref.shape[0]):
        free_top = free_top + metal_inv_ref[0, i] * metal_ref[i]

    for load in loads:
        load.wait()

    def gather(group, carry):
        base = pl.multiple_of(group * 8, 8)
        for k in range(8):
            col = col_ref[base + k]
            for c in range(3):
                rows[c, pl.ds(base + k, 1), :] = xv[c, pl.ds(col, 1), :]
        return carry

    lax.fori_loop(0, faces // 8, gather, 0)
    for side in range(2):
        for c in range(comps):
            for p in range(pitch_cells):
                at = p * span_cells + side * (span_cells - 1)
                edge_ref[side, c, p : p + 1, :] = xv[c, at : at + 1, :]

    lane = lax.broadcasted_iota(jnp.int32, (LANES, LANES), 1)
    for part in range(faces // LANES):
        at = slice(part * LANES, (part + 1) * LANES)
        low = jnp.broadcast_to(low_ref[part : part + 1, :], (LANES, LANES)).T
        index = low + (lane & (HALF - 1))
        far = index >= LANES
        index = index & (LANES - 1)

        def window(c):
            near = jnp.take_along_axis(rows[c, at, 0:LANES], index, axis=1)
            return jnp.where(
                far, jnp.take_along_axis(rows[c, at, LANES : 2 * LANES], index, axis=1), near
            )

        force = jnp.where(lane < HALF, window(0), window(1))
        speed = dot3(pieces(force, 2), table, NT)
        for step in range(PICARD):
            square = speed * speed
            damping = DRAG_COEF * lax.rsqrt(1.0 + square + pltpu.roll(square, HALF, 1))
            rest = pieces(force - damping * speed, 2)
            if step < PICARD - 1:
                speed = dot3(rest, table, NT)
        top_speed = dot3(top, rest, NT)
        fluid_top = dot3(top, pieces(window(2), 2), NT)
        conduct = coef_ref[0:1, at]
        viscosity = coef_ref[1:2, at]
        faces_ref[0:1, at] = viscosity * top_speed[0:1]
        faces_ref[1:2, at] = viscosity * top_speed[1:2]
        faces_ref[2:3, at] = fluid_top[0:1]
        faces_ref[3:4, at] = conduct
    faces_ref[4:5, :] = owner.astype(F32)
    faces_ref[5:6, :] = rank
    faces_ref[6:8, :] = jnp.zeros((2, faces), F32)

    conduct = faces_ref[3:4, :]
    heat = conduct * faces_ref[2:3, :]
    place = onehot(rank.astype(jnp.int32), HALF).astype(BF16)

    def slots(value, count):
        total = jnp.zeros((devices, HALF), F32)
        for part in pieces(value, count):
            total = total + dot((choose * part.astype(F32)).astype(BF16), place, NT)
        return total

    used = slots(jnp.ones_like(rank), 1)
    blank = jnp.zeros((devices, HALF), F32)

    def widen(value):
        if per_peer == HALF:
            return value
        return jnp.concatenate([value, jnp.zeros((devices, HALF - per_peer), F32)], axis=1)

    send_ref[pl.ds(0, devices, stride=8), :] = jnp.concatenate(
        [slots(heat, 3), slots(conduct, 3)], axis=1
    )
    send_ref[pl.ds(1, devices, stride=8), :] = jnp.concatenate([used, blank], axis=1)
    send_ref[pl.ds(2, devices, stride=8), :] = jnp.concatenate(
        [widen(free_top), widen(conduct_ref[...])], axis=1
    )
    empty = jnp.concatenate([blank, blank], axis=1)
    for j in range(3, 8):
        send_ref[pl.ds(j, devices, stride=8), :] = empty


def exchange_kernel(
    n_pitch,
    n_span,
    x_ref,
    edge_ref,
    tile_ref,
    got_ref,
    pitch_ref,
    span_ref,
    own_sem,
    tile_send,
    tile_recv,
    halo_send,
    halo_recv,
):
    devices = n_pitch * n_span
    pitch = lax.axis_index("pitch")
    span = lax.axis_index("span")
    me = pitch * n_span + span
    rows = x_ref.shape[1]
    barrier = pltpu.get_barrier_semaphore()

    def greet(k, carry):
        peer = lax.rem(me + k, devices)
        pl.semaphore_signal(
            barrier, inc=1, device_id=(peer // n_span, lax.rem(peer, n_span)), device_id_type=MESH
        )
        return carry

    lax.fori_loop(1, devices, greet, 0)
    pl.semaphore_wait(barrier, devices - 1)

    after = (lax.rem(pitch + 1, n_pitch), span)
    before = (lax.rem(pitch + n_pitch - 1, n_pitch), span)
    up = pltpu.make_async_remote_copy(
        src_ref=x_ref.at[:, rows - 1], dst_ref=pitch_ref.at[0], send_sem=halo_send.at[0],
        recv_sem=halo_recv.at[0], device_id=after, device_id_type=MESH,
    )
    down = pltpu.make_async_remote_copy(
        src_ref=x_ref.at[:, 0], dst_ref=pitch_ref.at[1], send_sem=halo_send.at[1],
        recv_sem=halo_recv.at[1], device_id=before, device_id_type=MESH,
    )
    right = pltpu.make_async_remote_copy(
        src_ref=edge_ref.at[1], dst_ref=span_ref.at[0], send_sem=halo_send.at[2],
        recv_sem=halo_recv.at[2], device_id=(pitch, lax.rem(span + 1, n_span)),
        device_id_type=MESH,
    )
    left = pltpu.make_async_remote_copy(
        src_ref=edge_ref.at[0], dst_ref=span_ref.at[1], send_sem=halo_send.at[3],
        recv_sem=halo_recv.at[3], device_id=(pitch, lax.rem(span + n_span - 1, n_span)),
        device_id_type=MESH,
    )
    up.start()
    down.start()

    @pl.when(span < n_span - 1)
    def _():
        right.start()

    @pl.when(span > 0)
    def _():
        left.start()

    def tile_copy(k):
        peer = lax.rem(me + k, devices)
        return pltpu.make_async_remote_copy(
            src_ref=tile_ref.at[pl.ds(pl.multiple_of(peer * 8, 8), 8), :],
            dst_ref=got_ref.at[pl.ds(pl.multiple_of(me * 8, 8), 8), :],
            send_sem=tile_send.at[k],
            recv_sem=tile_recv.at[k],
            device_id=(peer // n_span, lax.rem(peer, n_span)),
            device_id_type=MESH,
        )

    def tile_start(k, carry):
        tile_copy(k).start()
        return carry

    lax.fori_loop(1, devices, tile_start, 0)
    mine = pl.ds(pl.multiple_of(me * 8, 8), 8)
    own = pltpu.make_async_copy(tile_ref.at[mine, :], got_ref.at[mine, :], own_sem)
    own.start()

    @pl.when(span == 0)
    def _():
        span_ref[0] = jnp.zeros(span_ref.shape[1:], F32)

    @pl.when(span == n_span - 1)
    def _():
        span_ref[1] = jnp.zeros(span_ref.shape[1:], F32)

    own.wait()

    def tile_wait(k, carry):
        tile_copy(k).wait()
        return carry

    lax.fori_loop(1, devices, tile_wait, 0)
    up.wait()
    down.wait()

    @pl.when(span < n_span - 1)
    def _():
        right.wait_send()

    @pl.when(span > 0)
    def _():
        left.wait_send()

    @pl.when(span > 0)
    def _():
        right.wait_recv()

    @pl.when(span < n_span - 1)
    def _():
        left.wait_recv()


def advance_kernel(
    devices,
    per_peer,
    g_ref,
    metal_inv_ref,
    x_ref,
    prev_ref,
    next_ref,
    pitch_ref,
    span_ref,
    faces_ref,
    cell_ref,
    got_ref,
    metal_ref,
    conduct_ref,
    out_ref,
    metal_out_ref,
    wall,
):
    comp = pl.program_id(0)
    part = pl.program_id(1)
    parts = pl.num_programs(1)
    chunk, span_cells, normal = x_ref.shape[1:]
    pitch_cells = wall.shape[1] // 4
    fluid_factor = 1.0 - ALPHA_FLUID * g_ref[0, 0]
    metal_factor = 1.0 - BETA_METAL * metal_inv_ref[0, 0]

    @pl.when((comp == 0) & (part == 0))
    def _():
        rank = faces_ref[5:6, :].astype(jnp.int32)
        choose = onehot(faces_ref[4:5, :].astype(jnp.int32), devices).astype(BF16)
        picked = jnp.zeros((LANES, rank.shape[1]), F32)
        for piece in pieces(got_ref[pl.ds(2, devices, stride=8), :], 3):
            picked = picked + dot(piece, choose, TN)
        picked = picked * onehot(rank, LANES, HALF - 1)
        metal_top = jnp.sum(picked[0:HALF], axis=0, keepdims=True)
        conduct_metal = jnp.sum(picked[HALF:LANES], axis=0, keepdims=True)
        fluid_top = faces_ref[2:3, :]
        conduct = faces_ref[3:4, :]
        wall_temp = (conduct * fluid_top + conduct_metal * metal_top) / (
            conduct * fluid_factor + conduct_metal * metal_factor
        )
        heat = conduct * (fluid_top - fluid_factor * wall_temp)
        cell = cell_ref[...]
        at_pitch = onehot(cell // span_cells, pitch_cells)
        at_span = onehot(lax.rem(cell, span_cells), span_cells).astype(BF16)
        split = [pieces(v, 3) for v in (faces_ref[0:1, :], faces_ref[1:2, :], heat)]
        total = jnp.zeros(wall.shape, F32)
        for k in range(3):
            spread = [(at_pitch * s[k].astype(F32)).astype(BF16) for s in split]
            spread.append(jnp.zeros(at_pitch.shape, BF16))
            total = total + dot(at_span, jnp.concatenate(spread, axis=0), NT)
        wall[...] = -TIME_STEP * total

        first = got_ref[pl.ds(0, devices, stride=8), :]
        used = got_ref[pl.ds(1, devices, stride=8), :][:, 0:per_peer]
        flux = first[:, 0:per_peer]
        fluid = first[:, HALF : HALF + per_peer]
        metal_k = conduct_ref[...]
        order = metal_ref.shape[0]
        old = [metal_ref[i] for i in range(order)]

        def free(k):
            value = metal_inv_ref[k, 0] * old[0]
            for i in range(1, order):
                value = value + metal_inv_ref[k, i] * old[i]
            return value

        top = free(0)
        temp = (flux + metal_k * top) / (
            fluid * fluid_factor + metal_k * metal_factor + (1.0 - used)
        )
        for k in range(order):
            value = top if k == 0 else free(k)
            metal_out_ref[k] = jnp.where(
                used > 0.5, value + BETA_METAL * temp * metal_inv_ref[k, 0], old[k]
            )

    weight = TIME_STEP * DIFFUSION
    drift = TIME_STEP * ADVECTION * 0.5
    row = lax.broadcasted_iota(jnp.int32, (span_cells, normal), 0)
    lane = lax.broadcasted_iota(jnp.int32, (span_cells, normal), 1)
    lane_one = lax.broadcasted_iota(jnp.int32, (span_cells, LANES), 1)
    before = jnp.where(part == 0, pitch_ref[0, 0], prev_ref[0, 0])
    after = jnp.where(part == parts - 1, pitch_ref[1, 0], next_ref[0, 0])
    for p in range(chunk):
        here = x_ref[0, p]
        prev = before if p == 0 else x_ref[0, p - 1]
        post = after if p == chunk - 1 else x_ref[0, p + 1]
        span_prev = jnp.where(row == 0, span_ref[0, 0, p : p + 1, :], pltpu.roll(here, 1, 0))
        span_next = jnp.where(
            row == span_cells - 1, span_ref[1, 0, p : p + 1, :], pltpu.roll(here, span_cells - 1, 0)
        )
        down = jnp.where(lane == 0, here, pltpu.roll(here, 1, 1))
        up = jnp.where(lane == normal - 1, here, pltpu.roll(here, normal - 1, 1))
        value = (
            (1.0 - 6.0 * weight) * here
            + (weight - drift) * post
            + (weight + drift) * prev
            + weight * ((span_prev + span_next) + (down + up))
        )
        out_ref[0, p] = value
        column = comp * pitch_cells + part * chunk + p
        source = pltpu.roll(wall[...], lax.rem(LANES - column, LANES), 1)
        out_ref[0, p, :, 0:LANES] += jnp.where(lane_one == 0, source, 0.0)


def vmem():
    return pl.BlockSpec(memory_space=pltpu.VMEM)


def smem():
    return pl.BlockSpec(memory_space=pltpu.SMEM)


def local(
    n_pitch,
    n_span,
    flow_state,
    wall_inverse,
    metal_inverse,
    metal_state,
    metal_conduct,
    face_coef,
    owner_map,
    face_cell,
    sample_col,
    sample_low,
):
    devices = n_pitch * n_span
    comps, pitch_cells, span_cells, normal = flow_state.shape
    order, slot_dev = metal_state.shape
    per_peer = slot_dev // devices
    faces = owner_map.shape[0]
    metal = metal_state.reshape(order, devices, per_peer)
    conduct = metal_conduct.reshape(devices, per_peer)
    any_space = pl.BlockSpec(memory_space=pl.ANY)

    tiles, face_rows, edges = pl.pallas_call(
        functools.partial(sample_kernel, devices, per_peer, span_cells),
        out_shape=(
            jax.ShapeDtypeStruct((devices * 8, LANES), F32),
            jax.ShapeDtypeStruct((8, faces), F32),
            jax.ShapeDtypeStruct((2, comps, pitch_cells, normal), F32),
        ),
        in_specs=[smem(), smem(), any_space] + [vmem()] * 6,
        out_specs=[vmem()] * 3,
        scratch_shapes=[
            pltpu.VMEM((comps, pitch_cells * span_cells, normal), F32),
            pltpu.VMEM((3, faces, normal), F32),
            pltpu.VMEM((LANES, LANES), F32),
            pltpu.SemaphoreType.DMA((comps,)),
        ],
        compiler_params=pltpu.CompilerParams(vmem_limit_bytes=VMEM_LIMIT),
        name="sample_faces",
    )(
        sample_col,
        metal_inverse,
        flow_state.reshape(comps, pitch_cells * span_cells, normal),
        sample_low.reshape(faces // LANES, LANES),
        owner_map.reshape(1, faces),
        face_coef,
        wall_inverse,
        metal,
        conduct,
    )

    got, pitch_halo, span_halo = pl.pallas_call(
        functools.partial(exchange_kernel, n_pitch, n_span),
        out_shape=(
            jax.ShapeDtypeStruct((devices * 8, LANES), F32),
            jax.ShapeDtypeStruct((2, comps, span_cells, normal), F32),
            jax.ShapeDtypeStruct((2, comps, pitch_cells, normal), F32),
        ),
        in_specs=[any_space, vmem(), vmem()],
        out_specs=[vmem()] * 3,
        scratch_shapes=[
            pltpu.SemaphoreType.DMA,
            pltpu.SemaphoreType.DMA((devices,)),
            pltpu.SemaphoreType.DMA((devices,)),
            pltpu.SemaphoreType.DMA((4,)),
            pltpu.SemaphoreType.DMA((4,)),
        ],
        compiler_params=pltpu.CompilerParams(
            collective_id=0, has_side_effects=True, vmem_limit_bytes=VMEM_LIMIT
        ),
        name="exchange",
    )(flow_state, edges, tiles)

    chunk = pitch_cells // 2
    new_state, metal_out = pl.pallas_call(
        functools.partial(advance_kernel, devices, per_peer),
        grid=(comps, 2),
        out_shape=(
            jax.ShapeDtypeStruct(flow_state.shape, F32),
            jax.ShapeDtypeStruct(metal.shape, F32),
        ),
        in_specs=[
            smem(),
            smem(),
            pl.BlockSpec((1, chunk, span_cells, normal), lambda c, i: (c, i, 0, 0)),
            pl.BlockSpec(
                (1, 1, span_cells, normal),
                lambda c, i: (c, lax.rem(i * chunk + pitch_cells - 1, pitch_cells), 0, 0),
            ),
            pl.BlockSpec(
                (1, 1, span_cells, normal),
                lambda c, i: (c, lax.rem((i + 1) * chunk, pitch_cells), 0, 0),
            ),
            pl.BlockSpec((2, 1, span_cells, normal), lambda c, i: (0, c, 0, 0)),
            pl.BlockSpec((2, 1, chunk, normal), lambda c, i: (0, c, i, 0)),
            vmem(),
            vmem(),
            vmem(),
            vmem(),
            vmem(),
        ],
        out_specs=[
            pl.BlockSpec((1, chunk, span_cells, normal), lambda c, i: (c, i, 0, 0)),
            pl.BlockSpec(metal.shape, lambda c, i: (0, 0, 0)),
        ],
        scratch_shapes=[pltpu.VMEM((span_cells, 4 * pitch_cells), F32)],
        compiler_params=pltpu.CompilerParams(vmem_limit_bytes=VMEM_LIMIT),
        name="advance",
    )(
        wall_inverse,
        metal_inverse,
        flow_state,
        flow_state,
        flow_state,
        pitch_halo,
        span_halo,
        face_rows,
        face_cell.reshape(1, faces),
        got,
        metal,
        conduct,
    )
    return (new_state, metal_out.reshape(order, slot_dev))


def solution(mesh):
    return jax.shard_map(
        functools.partial(local, mesh.shape["pitch"], mesh.shape["span"]),
        mesh=mesh,
        in_specs=(
            P(None, "pitch", "span", None),
            P(),
            P(),
            P(None, ("pitch", "span")),
            P(("pitch", "span")),
            P(None, ("pitch", "span")),
            P(("pitch", "span"), None),
            P(("pitch", "span")),
            P(("pitch", "span")),
            P(("pitch", "span")),
        ),
        out_specs=(P(None, "pitch", "span", None), P(None, ("pitch", "span"))),
        check_vma=False,
    )
```

```python
import functools
import jax
import jax.numpy as jnp
from jax import lax
from jax.experimental import pallas as pl
from jax.experimental.pallas import tpu as pltpu
from jax.sharding import PartitionSpec as P

PICARD = 3
ALPHA_FLUID = 0.5
BETA_METAL = 0.5
DRAG_COEF = 0.5
TIME_STEP = 0.5
DIFFUSION = 0.2
ADVECTION = 0.6
HALF = 64
LANES = 128
F32 = jnp.float32
BF16 = jnp.bfloat16
VMEM_LIMIT = 56 * 1024 * 1024
MESH = pl.DeviceIdType.MESH

NN = (((1,), (0,)), ((), ()))
NT = (((1,), (1,)), ((), ()))
TN = (((0,), (0,)), ((), ()))


def pieces(value, count):
    out = []
    for _ in range(count):
        part = value.astype(BF16)
        out.append(part)
        value = value - part.astype(F32)
    return out


def dot(a, b, dims):
    return lax.dot_general(a, b, dims, preferred_element_type=F32)


def dot3(a, b, dims):
    (a1, a2), (b1, b2) = (a, b)
    return dot(a1, b1, dims) + (dot(a1, b2, dims) + dot(a2, b1, dims))


def onehot(row, count, mask=None):
    index = lax.broadcasted_iota(jnp.int32, (count, row.shape[1]), 0)
    if mask is not None:
        index = index & mask
    return jnp.where(index == row, 1.0, 0.0).astype(F32)


def sample_kernel(
    n_pitch,
    n_span,
    per_peer,
    span_cells,
    col_ref,
    low_smem,
    g_smem,
    metal_smem,
    x_ref,
    low_ref,
    owner_ref,
    cell_ref,
    coef_ref,
    g_ref,
    metal_inv_ref,
    metal_ref,
    conduct_ref,
    wall_ref,
    metal_out_ref,
    pitch_ref,
    span_ref,
    xv,
    rows,
    gg,
    speed_rows,
    edges,
    offer,
    offer_got,
    reply,
    reply_got,
    slot_rows,
    load_sem,
    tile_send,
    tile_recv,
    halo_send,
    halo_recv,
):
    devices = n_pitch * n_span
    pitch = lax.axis_index("pitch")
    span = lax.axis_index("span")
    me = pitch * n_span + span
    comps = x_ref.shape[0]
    columns = x_ref.shape[1]
    pitch_cells = columns // span_cells
    faces = rows.shape[1]
    slot_dev = metal_ref.shape[1]
    per_tile = LANES // per_peer
    barrier = pltpu.get_barrier_semaphore()

    def wrap(value, size):
        return jnp.where(value >= size, value - size, value)

    def each_peer(visit):
        for d in range(1, n_span):
            visit(pitch, wrap(span + d, n_span))

        def ring(step, carry):
            other = wrap(pitch + step, n_pitch)
            for d in range(n_span):
                visit(other, wrap(span + d, n_span))
            return carry

        lax.fori_loop(1, n_pitch, ring, 0)

    each_peer(
        lambda p, s: pl.semaphore_signal(barrier, inc=1, device_id=(p, s), device_id_type=MESH)
    )
    loads = [
        pltpu.make_async_copy(
            x_ref.at[c, :, pl.ds(t * LANES, LANES)], xv.at[c, t], load_sem.at[c, t]
        )
        for c in range(comps)
        for t in range(2)
    ]
    for load in loads:
        load.start()

    old = metal_ref[...]
    free = dot3(pieces(metal_inv_ref[...], 2), pieces(old, 2), NN)
    offer[0:1, :] = free[0:1]
    offer[1:2, :] = conduct_ref[...]
    offer[2:8, :] = jnp.zeros((6, slot_dev), F32)

    pl.semaphore_wait(barrier, devices - 1)
    up = pltpu.make_async_remote_copy(
        src_ref=x_ref.at[:, pl.ds(columns - span_cells, span_cells)], dst_ref=pitch_ref.at[0],
        send_sem=halo_send.at[0], recv_sem=halo_recv.at[0],
        device_id=(wrap(pitch + 1, n_pitch), span), device_id_type=MESH,
    )
    down = pltpu.make_async_remote_copy(
        src_ref=x_ref.at[:, pl.ds(0, span_cells)], dst_ref=pitch_ref.at[1],
        send_sem=halo_send.at[1], recv_sem=halo_recv.at[1],
        device_id=(wrap(pitch + n_pitch - 1, n_pitch), span), device_id_type=MESH,
    )
    right = pltpu.make_async_remote_copy(
        src_ref=edges.at[1], dst_ref=span_ref.at[0],
        send_sem=halo_send.at[2], recv_sem=halo_recv.at[2],
        device_id=(pitch, wrap(span + 1, n_span)), device_id_type=MESH,
    )
    left = pltpu.make_async_remote_copy(
        src_ref=edges.at[0], dst_ref=span_ref.at[1],
        send_sem=halo_send.at[3], recv_sem=halo_recv.at[3],
        device_id=(pitch, wrap(span + n_span - 1, n_span)), device_id_type=MESH,
    )
    up.start()
    down.start()
    mine = pl.ds(pl.multiple_of(me * 8, 8), 8)

    def offer_of(index):
        return offer.at[:, pl.ds(pl.multiple_of(index // per_tile * LANES, LANES), LANES)]

    def offer_start(p, s):
        pltpu.make_async_remote_copy(
            src_ref=offer_of(p * n_span + s), dst_ref=offer_got.at[mine, :],
            send_sem=tile_send.at[0], recv_sem=tile_recv.at[0],
            device_id=(p, s), device_id_type=MESH,
        ).start()

    each_peer(offer_start)
    offer_got[mine, :] = offer[
        :, pl.ds(pl.multiple_of(me // per_tile * LANES, LANES), LANES)
    ]

    gg[...] = jnp.zeros_like(gg)
    gg[0:HALF, 0:HALF] = g_ref[...]
    gg[HALF:LANES, HALF:LANES] = g_ref[...]
    table_hi, table_lo = pieces(gg[...], 2)
    both = jnp.concatenate([table_hi, table_hi], axis=1)
    single = jnp.concatenate([table_lo, jnp.zeros_like(table_lo)], axis=1)
    table = jnp.concatenate([both, single], axis=0)
    row_pick = lax.broadcasted_iota(jnp.int32, (8, LANES), 0)
    top_u = jnp.broadcast_to(gg[0:1, :], (8, LANES))
    top_w = jnp.broadcast_to(gg[HALF : HALF + 1, :], (8, LANES))
    top = pieces(jnp.where(row_pick == 0, top_u, jnp.where(row_pick == 1, top_w, 0.0)), 2)

    choose = onehot(owner_ref[...], devices)
    choose_b = choose.astype(BF16)
    up_row = lax.broadcasted_iota(jnp.int32, (LANES, LANES), 0)
    up_col = lax.broadcasted_iota(jnp.int32, (LANES, LANES), 1)
    upper = jnp.where(up_row < up_col, 1.0, 0.0).astype(BF16)
    running = jnp.zeros((devices, 1), F32)
    ranks = []
    for start in range(0, faces, LANES):
        block = choose[:, start : start + LANES]
        prior = dot(choose_b[:, start : start + LANES], upper, NN) + running
        ranks.append(jnp.sum(prior * block, axis=0, keepdims=True))
        running = running + jnp.sum(block, axis=1, keepdims=True)
    lane_at = (me & (per_tile - 1)) * per_peer
    rank = jnp.concatenate(ranks, axis=1).astype(jnp.int32) + lane_at
    place = onehot(rank, LANES)
    place_b = place.astype(BF16)

    for load in loads:
        load.wait()

    for side in range(2):
        for c in range(comps):
            for p in range(pitch_cells):
                at = p * span_cells + side * (span_cells - 1)
                for t in range(2):
                    edges[side, c, p : p + 1, t * LANES : (t + 1) * LANES] = xv[c, t, at : at + 1, :]

    @pl.when(span < n_span - 1)
    def _():
        right.start()

    @pl.when(span > 0)
    def _():
        left.start()

    @pl.when(span == 0)
    def _():
        span_ref[0] = jnp.zeros(span_ref.shape[1:], F32)

    @pl.when(span == n_span - 1)
    def _():
        span_ref[1] = jnp.zeros(span_ref.shape[1:], F32)

    lane_row = lax.broadcasted_iota(jnp.int32, (1, LANES), 1)

    def gather(group, carry):
        base = pl.multiple_of(group * 8, 8)
        for k in range(8):
            col = col_ref[base + k]
            low = low_smem[base + k]
            near = low >> 7
            far = (low + HALF - 1) >> 7
            keep = lane_row >= (low & (LANES - 1))
            for c in range(3):
                rows[c, pl.ds(base + k, 1), :] = jnp.where(
                    keep, xv[c, near, pl.ds(col, 1), :], xv[c, far, pl.ds(col, 1), :]
                )
        return carry

    lax.fori_loop(0, faces // 8, gather, 0)

    lane = lax.broadcasted_iota(jnp.int32, (LANES, LANES), 1)
    force = []
    warm = []
    for part in range(faces // LANES):
        at = slice(part * LANES, (part + 1) * LANES)
        low = jnp.broadcast_to(low_ref[part : part + 1, :], (LANES, LANES)).T
        index = (low + (lane & (HALF - 1))) & (LANES - 1)
        window = [jnp.take_along_axis(rows[c, at, :], index, axis=1) for c in range(3)]
        force.append(jnp.where(lane < HALF, window[0], window[1]))
        warm.append(window[2])
    force = jnp.concatenate(force, axis=0)
    warm = jnp.concatenate(warm, axis=0)

    def solve(value):
        out = dot(jnp.concatenate(pieces(value, 2), axis=1), table, NT)
        return out[:, 0:LANES] + out[:, LANES : 2 * LANES]

    speed = solve(force)
    for step in range(PICARD):
        square = speed * speed
        damping = DRAG_COEF * lax.rsqrt(1.0 + square + pltpu.roll(square, HALF, 1))
        rest = force - damping * speed
        if step < PICARD - 1:
            speed = solve(rest)
    speed_rows[...] = dot3(top, pieces(rest, 2), NT)
    fluid_top = dot3(top, pieces(warm, 2), NT)[0:1]
    conduct = coef_ref[0:1, :]
    viscosity = coef_ref[1:2, :]

    spread = []
    for value in (conduct * fluid_top, conduct):
        spread += [(choose * part.astype(F32)).astype(BF16) for part in pieces(value, 3)]
    spread.append(choose_b)
    packed = dot(jnp.concatenate(spread, axis=0), place_b, NT)
    packed = [packed[k * devices : (k + 1) * devices] for k in range(7)]
    reply[pl.ds(0, devices, stride=8), :] = packed[0] + (packed[1] + packed[2])
    reply[pl.ds(1, devices, stride=8), :] = packed[3] + (packed[4] + packed[5])
    reply[pl.ds(2, devices, stride=8), :] = packed[6]
    for j in range(3, 8):
        reply[pl.ds(j, devices, stride=8), :] = jnp.zeros((devices, LANES), F32)

    def reply_start(p, s):
        index = p * n_span + s
        pltpu.make_async_remote_copy(
            src_ref=reply.at[pl.ds(pl.multiple_of(index * 8, 8), 8), :],
            dst_ref=reply_got.at[mine, :],
            send_sem=tile_send.at[1], recv_sem=tile_recv.at[1],
            device_id=(p, s), device_id_type=MESH,
        ).start()

    each_peer(reply_start)
    reply_got[mine, :] = reply[mine, :]

    def tiles_wait(k, src, dst):
        many = pl.ds(0, (devices - 1) * 8)
        pltpu.make_async_remote_copy(
            src_ref=src.at[many, :], dst_ref=dst.at[many, :],
            send_sem=tile_send.at[k], recv_sem=tile_recv.at[k],
            device_id=(wrap(pitch + 1, n_pitch), span), device_id_type=MESH,
        ).wait()

    fluid_factor = 1.0 - ALPHA_FLUID * g_smem[0, 0]
    metal_factor = 1.0 - BETA_METAL * metal_smem[0, 0]
    tiles_wait(0, reply, offer_got)
    thrice = jnp.concatenate([choose_b] * 3, axis=0)

    def from_owner(j):
        parts = pieces(offer_got[pl.ds(j, devices, stride=8), :], 3)
        return jnp.sum(
            dot(jnp.concatenate(parts, axis=0), thrice, TN) * place, axis=0, keepdims=True
        )

    metal_top = from_owner(0)
    conduct_metal = from_owner(1)
    wall_temp = (conduct * fluid_top + conduct_metal * metal_top) / (
        conduct * fluid_factor + conduct_metal * metal_factor
    )
    heat = conduct * (fluid_top - fluid_factor * wall_temp)
    cell = cell_ref[...]
    at_pitch = onehot(cell // span_cells, pitch_cells)
    at_span = onehot(lax.rem(cell, span_cells), span_cells).astype(BF16)
    fluxes = (viscosity * speed_rows[0:1, :], viscosity * speed_rows[1:2, :], heat)
    split = [pieces(v, 3) for v in fluxes]
    blank = jnp.zeros(at_pitch.shape, BF16)
    stack = []
    for k in range(3):
        stack += [(at_pitch * s[k].astype(F32)).astype(BF16) for s in split] + [blank]
    total = dot(at_span, jnp.concatenate(stack, axis=0), NT)
    wide = 4 * pitch_cells
    wall_ref[...] = -TIME_STEP * (
        total[:, 0:wide] + (total[:, wide : 2 * wide] + total[:, 2 * wide : 3 * wide])
    )

    tiles_wait(1, reply, reply_got)
    for t in range(slot_dev // LANES):
        tile = reply_got[t * per_tile * 8 : t * per_tile * 8 + 8, :]
        for k in range(t * per_tile + 1, (t + 1) * per_tile):
            tile = tile + reply_got[k * 8 : k * 8 + 8, :]
        slot_rows[:, t * LANES : (t + 1) * LANES] = tile
    metal_k = offer[1:2, :]
    used = slot_rows[2:3, :]
    temp = (slot_rows[0:1, :] + metal_k * offer[0:1, :]) / (
        slot_rows[1:2, :] * fluid_factor + metal_k * metal_factor + (1.0 - used)
    )
    metal_out_ref[...] = jnp.where(
        used > 0.5, free + BETA_METAL * metal_inv_ref[:, 0:1] * temp, old
    )

    up.wait()
    down.wait()

    @pl.when(span < n_span - 1)
    def _():
        right.wait_send()

    @pl.when(span > 0)
    def _():
        left.wait_send()

    @pl.when(span > 0)
    def _():
        right.wait_recv()

    @pl.when(span < n_span - 1)
    def _():
        left.wait_recv()


def advance_kernel(
    x_ref,
    prev_ref,
    next_ref,
    pitch_ref,
    span_ref,
    wall_ref,
    metal_ref,
    out_ref,
    metal_out_ref,
):
    comp = pl.program_id(0)
    part = pl.program_id(1)
    parts = pl.num_programs(1)
    chunk, span_cells, normal = x_ref.shape[1:]
    pitch_cells = wall_ref.shape[1] // 4

    @pl.when((comp == 0) & (part == 0))
    def _():
        metal_out_ref[...] = metal_ref[...]

    weight = TIME_STEP * DIFFUSION
    drift = TIME_STEP * ADVECTION * 0.5
    row = lax.broadcasted_iota(jnp.int32, (span_cells, normal), 0)
    lane = lax.broadcasted_iota(jnp.int32, (span_cells, normal), 1)
    lane_one = lax.broadcasted_iota(jnp.int32, (span_cells, LANES), 1)
    before = jnp.where(part == 0, pitch_ref[0, 0], prev_ref[0, 0])
    after = jnp.where(part == parts - 1, pitch_ref[1, 0], next_ref[0, 0])
    for p in range(chunk):
        here = x_ref[0, p]
        prev = before if p == 0 else x_ref[0, p - 1]
        post = after if p == chunk - 1 else x_ref[0, p + 1]
        span_prev = jnp.where(row == 0, span_ref[0, 0, p : p + 1, :], pltpu.roll(here, 1, 0))
        span_next = jnp.where(
            row == span_cells - 1, span_ref[1, 0, p : p + 1, :], pltpu.roll(here, span_cells - 1, 0)
        )
        down = jnp.where(lane == 0, here, pltpu.roll(here, 1, 1))
        up = jnp.where(lane == normal - 1, here, pltpu.roll(here, normal - 1, 1))
        value = (
            (1.0 - 6.0 * weight) * here
            + (weight - drift) * post
            + (weight + drift) * prev
            + weight * ((span_prev + span_next) + (down + up))
        )
        out_ref[0, p] = value
        column = comp * pitch_cells + part * chunk + p
        source = pltpu.roll(wall_ref[...], lax.rem(LANES - column, LANES), 1)
        out_ref[0, p, :, 0:LANES] += jnp.where(lane_one == 0, source, 0.0)


def vmem():
    return pl.BlockSpec(memory_space=pltpu.VMEM)


def smem():
    return pl.BlockSpec(memory_space=pltpu.SMEM)


def local(
    n_pitch,
    n_span,
    flow_state,
    wall_inverse,
    metal_inverse,
    metal_state,
    metal_conduct,
    face_coef,
    owner_map,
    face_cell,
    sample_col,
    sample_low,
):
    devices = n_pitch * n_span
    comps, pitch_cells, span_cells, normal = flow_state.shape
    slot_dev = metal_state.shape[1]
    per_peer = slot_dev // devices
    faces = owner_map.shape[0]
    any_space = pl.BlockSpec(memory_space=pl.ANY)

    wall, metal_new, pitch_halo, span_halo = pl.pallas_call(
        functools.partial(sample_kernel, n_pitch, n_span, per_peer, span_cells),
        out_shape=(
            jax.ShapeDtypeStruct((span_cells, 4 * pitch_cells), F32),
            jax.ShapeDtypeStruct(metal_state.shape, F32),
            jax.ShapeDtypeStruct((2, comps, span_cells, normal), F32),
            jax.ShapeDtypeStruct((2, comps, pitch_cells, normal), F32),
        ),
        in_specs=[smem()] * 4 + [any_space] + [vmem()] * 8,
        out_specs=[vmem()] * 4,
        scratch_shapes=[
            pltpu.VMEM((comps, 2, pitch_cells * span_cells, LANES), F32),
            pltpu.VMEM((3, faces, LANES), F32),
            pltpu.VMEM((LANES, LANES), F32),
            pltpu.VMEM((8, faces), F32),
            pltpu.VMEM((2, comps, pitch_cells, normal), F32),
            pltpu.VMEM((8, slot_dev), F32),
            pltpu.VMEM((devices * 8, LANES), F32),
            pltpu.VMEM((devices * 8, LANES), F32),
            pltpu.VMEM((devices * 8, LANES), F32),
            pltpu.VMEM((8, slot_dev), F32),
            pltpu.SemaphoreType.DMA((comps, 2)),
            pltpu.SemaphoreType.DMA((2,)),
            pltpu.SemaphoreType.DMA((2,)),
            pltpu.SemaphoreType.DMA((4,)),
            pltpu.SemaphoreType.DMA((4,)),
        ],
        compiler_params=pltpu.CompilerParams(
            collective_id=0, has_side_effects=True, vmem_limit_bytes=VMEM_LIMIT
        ),
        name="sample_faces",
    )(
        sample_col,
        sample_low,
        wall_inverse,
        metal_inverse,
        flow_state.reshape(comps, pitch_cells * span_cells, normal),
        sample_low.reshape(faces // LANES, LANES),
        owner_map.reshape(1, faces),
        face_cell.reshape(1, faces),
        face_coef,
        wall_inverse,
        metal_inverse,
        metal_state,
        metal_conduct.reshape(1, slot_dev),
    )

    chunk = pitch_cells // 2
    new_state, metal_out = pl.pallas_call(
        advance_kernel,
        grid=(comps, 2),
        out_shape=(
            jax.ShapeDtypeStruct(flow_state.shape, F32),
            jax.ShapeDtypeStruct(metal_state.shape, F32),
        ),
        in_specs=[
            pl.BlockSpec((1, chunk, span_cells, normal), lambda c, i: (c, i, 0, 0)),
            pl.BlockSpec(
                (1, 1, span_cells, normal),
                lambda c, i: (c, lax.rem(i * chunk + pitch_cells - 1, pitch_cells), 0, 0),
            ),
            pl.BlockSpec(
                (1, 1, span_cells, normal),
                lambda c, i: (c, lax.rem((i + 1) * chunk, pitch_cells), 0, 0),
            ),
            pl.BlockSpec((2, 1, span_cells, normal), lambda c, i: (0, c, 0, 0)),
            pl.BlockSpec((2, 1, chunk, normal), lambda c, i: (0, c, i, 0)),
            vmem(),
            vmem(),
        ],
        out_specs=[
            pl.BlockSpec((1, chunk, span_cells, normal), lambda c, i: (c, i, 0, 0)),
            pl.BlockSpec(metal_state.shape, lambda c, i: (0, 0)),
        ],
        compiler_params=pltpu.CompilerParams(vmem_limit_bytes=VMEM_LIMIT),
        name="advance",
    )(
        flow_state,
        flow_state,
        flow_state,
        pitch_halo,
        span_halo,
        wall,
        metal_new,
    )
    return (new_state, metal_out)


def solution(mesh):
    return jax.shard_map(
        functools.partial(local, mesh.shape["pitch"], mesh.shape["span"]),
        mesh=mesh,
        in_specs=(
            P(None, "pitch", "span", None),
            P(),
            P(),
            P(None, ("pitch", "span")),
            P(("pitch", "span")),
            P(None, ("pitch", "span")),
            P(("pitch", "span"), None),
            P(("pitch", "span")),
            P(("pitch", "span")),
            P(("pitch", "span")),
        ),
        out_specs=(P(None, "pitch", "span", None), P(None, ("pitch", "span"))),
        check_vma=False,
    )
```

```python
import functools
import jax
import jax.numpy as jnp
from jax import lax
from jax.experimental import pallas as pl
from jax.experimental.pallas import tpu as pltpu
from jax.sharding import PartitionSpec as P

PICARD = 3
ALPHA_FLUID = 0.5
BETA_METAL = 0.5
DRAG_COEF = 0.5
TIME_STEP = 0.5
DIFFUSION = 0.2
ADVECTION = 0.6
HALF = 64
LANES = 128
F32 = jnp.float32
BF16 = jnp.bfloat16
VMEM_LIMIT = 56 * 1024 * 1024
MESH = pl.DeviceIdType.MESH

NN = (((1,), (0,)), ((), ()))
NT = (((1,), (1,)), ((), ()))
TN = (((0,), (0,)), ((), ()))


def pieces(value, count):
    out = []
    for _ in range(count):
        part = value.astype(BF16)
        out.append(part)
        value = value - part.astype(F32)
    return out


def dot(a, b, dims):
    return lax.dot_general(a, b, dims, preferred_element_type=F32)


def dot3(a, b, dims):
    (a1, a2), (b1, b2) = (a, b)
    return dot(a1, b1, dims) + (dot(a1, b2, dims) + dot(a2, b1, dims))


def onehot(row, count, mask=None):
    index = lax.broadcasted_iota(jnp.int32, (count, row.shape[1]), 0)
    if mask is not None:
        index = index & mask
    return jnp.where(index == row, 1.0, 0.0).astype(F32)


def sample_kernel(
    n_pitch,
    n_span,
    per_peer,
    span_cells,
    col_ref,
    low_smem,
    g_smem,
    metal_smem,
    x_ref,
    low_ref,
    owner_ref,
    cell_ref,
    coef_ref,
    g_ref,
    metal_inv_ref,
    metal_ref,
    conduct_ref,
    wall_ref,
    metal_out_ref,
    pitch_ref,
    span_ref,
    xv,
    rows,
    gg,
    speed_rows,
    edges,
    offer,
    offer_got,
    reply,
    reply_got,
    slot_rows,
    load_sem,
    tile_send,
    tile_recv,
    halo_send,
    halo_recv,
):
    devices = n_pitch * n_span
    pitch = lax.axis_index("pitch")
    span = lax.axis_index("span")
    me = pitch * n_span + span
    comps = x_ref.shape[0]
    columns = x_ref.shape[1]
    pitch_cells = columns // span_cells
    faces = rows.shape[0] // 8
    slot_dev = metal_ref.shape[1]
    per_tile = LANES // per_peer
    barrier = pltpu.get_barrier_semaphore()

    def wrap(value, size):
        return jnp.where(value >= size, value - size, value)

    def each_peer(visit):
        for d in range(1, n_span):
            visit(pitch, wrap(span + d, n_span))

        def ring(step, carry):
            other = wrap(pitch + step, n_pitch)
            for d in range(n_span):
                visit(other, wrap(span + d, n_span))
            return carry

        lax.fori_loop(1, n_pitch, ring, 0)

    each_peer(
        lambda p, s: pl.semaphore_signal(barrier, inc=1, device_id=(p, s), device_id_type=MESH)
    )
    loads = [
        pltpu.make_async_copy(
            x_ref.at[c, :, pl.ds(t * LANES, LANES)],
            xv.at[pl.ds((c * 2 + t) * columns, columns), :],
            load_sem.at[c, t],
        )
        for c in range(comps)
        for t in range(2)
    ]
    for load in loads:
        load.start()

    old = metal_ref[...]
    free = dot3(pieces(metal_inv_ref[...], 2), pieces(old, 2), NN)
    offer[0:1, :] = free[0:1]
    offer[1:2, :] = conduct_ref[...]
    offer[2:8, :] = jnp.zeros((6, slot_dev), F32)

    pl.semaphore_wait(barrier, devices - 1)
    up = pltpu.make_async_remote_copy(
        src_ref=x_ref.at[:, pl.ds(columns - span_cells, span_cells)], dst_ref=pitch_ref.at[0],
        send_sem=halo_send.at[0], recv_sem=halo_recv.at[0],
        device_id=(wrap(pitch + 1, n_pitch), span), device_id_type=MESH,
    )
    down = pltpu.make_async_remote_copy(
        src_ref=x_ref.at[:, pl.ds(0, span_cells)], dst_ref=pitch_ref.at[1],
        send_sem=halo_send.at[1], recv_sem=halo_recv.at[1],
        device_id=(wrap(pitch + n_pitch - 1, n_pitch), span), device_id_type=MESH,
    )
    right = pltpu.make_async_remote_copy(
        src_ref=edges.at[1], dst_ref=span_ref.at[0],
        send_sem=halo_send.at[2], recv_sem=halo_recv.at[2],
        device_id=(pitch, wrap(span + 1, n_span)), device_id_type=MESH,
    )
    left = pltpu.make_async_remote_copy(
        src_ref=edges.at[0], dst_ref=span_ref.at[1],
        send_sem=halo_send.at[3], recv_sem=halo_recv.at[3],
        device_id=(pitch, wrap(span + n_span - 1, n_span)), device_id_type=MESH,
    )
    up.start()
    down.start()
    mine = pl.ds(pl.multiple_of(me * 8, 8), 8)

    def offer_of(index):
        return offer.at[:, pl.ds(pl.multiple_of(index // per_tile * LANES, LANES), LANES)]

    def offer_start(p, s):
        pltpu.make_async_remote_copy(
            src_ref=offer_of(p * n_span + s), dst_ref=offer_got.at[mine, :],
            send_sem=tile_send.at[0], recv_sem=tile_recv.at[0],
            device_id=(p, s), device_id_type=MESH,
        ).start()

    each_peer(offer_start)
    offer_got[mine, :] = offer[
        :, pl.ds(pl.multiple_of(me // per_tile * LANES, LANES), LANES)
    ]

    gg[...] = jnp.zeros_like(gg)
    gg[0:HALF, 0:HALF] = g_ref[...]
    gg[HALF:LANES, HALF:LANES] = g_ref[...]
    table_hi, table_lo = pieces(gg[...], 2)
    both = jnp.concatenate([table_hi, table_hi], axis=1)
    single = jnp.concatenate([table_lo, jnp.zeros_like(table_lo)], axis=1)
    table = jnp.concatenate([both, single], axis=0)
    row_pick = lax.broadcasted_iota(jnp.int32, (8, LANES), 0)
    top_u = jnp.broadcast_to(gg[0:1, :], (8, LANES))
    top_w = jnp.broadcast_to(gg[HALF : HALF + 1, :], (8, LANES))
    top = pieces(jnp.where(row_pick == 0, top_u, jnp.where(row_pick == 1, top_w, 0.0)), 2)

    choose = onehot(owner_ref[...], devices)
    choose_b = choose.astype(BF16)
    up_row = lax.broadcasted_iota(jnp.int32, (LANES, LANES), 0)
    up_col = lax.broadcasted_iota(jnp.int32, (LANES, LANES), 1)
    upper = jnp.where(up_row < up_col, 1.0, 0.0).astype(BF16)
    running = jnp.zeros((devices, 1), F32)
    ranks = []
    for start in range(0, faces, LANES):
        block = choose[:, start : start + LANES]
        prior = dot(choose_b[:, start : start + LANES], upper, NN) + running
        ranks.append(jnp.sum(prior * block, axis=0, keepdims=True))
        running = running + jnp.sum(block, axis=1, keepdims=True)
    lane_at = (me & (per_tile - 1)) * per_peer
    rank = jnp.concatenate(ranks, axis=1).astype(jnp.int32) + lane_at
    place = onehot(rank, LANES)
    place_b = place.astype(BF16)

    for load in loads:
        load.wait()

    for side in range(2):
        for c in range(comps):
            for t in range(2):
                at = (c * 2 + t) * columns + side * (span_cells - 1)
                edges[side, c, :, t * LANES : (t + 1) * LANES] = xv[
                    pl.ds(at, pitch_cells, stride=span_cells), :
                ]

    @pl.when(span < n_span - 1)
    def _():
        right.start()

    @pl.when(span > 0)
    def _():
        left.start()

    @pl.when(span == 0)
    def _():
        span_ref[0] = jnp.zeros(span_ref.shape[1:], F32)

    @pl.when(span == n_span - 1)
    def _():
        span_ref[1] = jnp.zeros(span_ref.shape[1:], F32)

    def gather(group, carry):
        base = group * 8
        for k in range(8):
            at = pl.multiple_of((base + k) * 8, 8)
            rows[pl.ds(at, 8), :] = xv[pl.ds(col_ref[base + k], 8, stride=columns), :]
        return carry

    lax.fori_loop(0, faces // 8, gather, 0)

    lane = lax.broadcasted_iota(jnp.int32, (LANES, LANES), 1)
    force = []
    warm = []
    for part in range(faces // LANES):
        low = jnp.broadcast_to(low_ref[part : part + 1, :], (LANES, LANES)).T
        index = (low + (lane & (HALF - 1))) & (LANES - 1)
        near = lane >= low
        window = []
        for c in range(3):
            first = rows[pl.ds(part * LANES * 8 + c * 2, LANES, stride=8), :]
            second = rows[pl.ds(part * LANES * 8 + c * 2 + 1, LANES, stride=8), :]
            window.append(jnp.take_along_axis(jnp.where(near, first, second), index, axis=1))
        force.append(jnp.where(lane < HALF, window[0], window[1]))
        warm.append(window[2])
    force = jnp.concatenate(force, axis=0)
    warm = jnp.concatenate(warm, axis=0)

    def solve(value):
        out = dot(jnp.concatenate(pieces(value, 2), axis=1), table, NT)
        return out[:, 0:LANES] + out[:, LANES : 2 * LANES]

    speed = solve(force)
    for step in range(PICARD):
        square = speed * speed
        damping = DRAG_COEF * lax.rsqrt(1.0 + square + pltpu.roll(square, HALF, 1))
        rest = force - damping * speed
        if step < PICARD - 1:
            speed = solve(rest)
    speed_rows[...] = dot3(top, pieces(rest, 2), NT)
    fluid_top = dot3(top, pieces(warm, 2), NT)[0:1]
    conduct = coef_ref[0:1, :]
    viscosity = coef_ref[1:2, :]

    spread = []
    for value in (conduct * fluid_top, conduct):
        spread += [(choose * part.astype(F32)).astype(BF16) for part in pieces(value, 3)]
    spread.append(choose_b)
    packed = dot(jnp.concatenate(spread, axis=0), place_b, NT)
    packed = [packed[k * devices : (k + 1) * devices] for k in range(7)]
    reply[pl.ds(0, devices, stride=8), :] = packed[0] + (packed[1] + packed[2])
    reply[pl.ds(1, devices, stride=8), :] = packed[3] + (packed[4] + packed[5])
    reply[pl.ds(2, devices, stride=8), :] = packed[6]
    for j in range(3, 8):
        reply[pl.ds(j, devices, stride=8), :] = jnp.zeros((devices, LANES), F32)

    def reply_start(p, s):
        index = p * n_span + s
        pltpu.make_async_remote_copy(
            src_ref=reply.at[pl.ds(pl.multiple_of(index * 8, 8), 8), :],
            dst_ref=reply_got.at[mine, :],
            send_sem=tile_send.at[1], recv_sem=tile_recv.at[1],
            device_id=(p, s), device_id_type=MESH,
        ).start()

    each_peer(reply_start)
    reply_got[mine, :] = reply[mine, :]

    def tiles_wait(k, src, dst):
        many = pl.ds(0, (devices - 1) * 8)
        pltpu.make_async_remote_copy(
            src_ref=src.at[many, :], dst_ref=dst.at[many, :],
            send_sem=tile_send.at[k], recv_sem=tile_recv.at[k],
            device_id=(wrap(pitch + 1, n_pitch), span), device_id_type=MESH,
        ).wait()

    fluid_factor = 1.0 - ALPHA_FLUID * g_smem[0, 0]
    metal_factor = 1.0 - BETA_METAL * metal_smem[0, 0]
    tiles_wait(0, reply, offer_got)
    thrice = jnp.concatenate([choose_b] * 3, axis=0)

    def from_owner(j):
        parts = pieces(offer_got[pl.ds(j, devices, stride=8), :], 3)
        return jnp.sum(
            dot(jnp.concatenate(parts, axis=0), thrice, TN) * place, axis=0, keepdims=True
        )

    metal_top = from_owner(0)
    conduct_metal = from_owner(1)
    wall_temp = (conduct * fluid_top + conduct_metal * metal_top) / (
        conduct * fluid_factor + conduct_metal * metal_factor
    )
    heat = conduct * (fluid_top - fluid_factor * wall_temp)
    cell = cell_ref[...]
    at_pitch = onehot(cell // span_cells, pitch_cells)
    at_span = onehot(lax.rem(cell, span_cells), span_cells).astype(BF16)
    fluxes = (viscosity * speed_rows[0:1, :], viscosity * speed_rows[1:2, :], heat)
    split = [pieces(v, 3) for v in fluxes]
    blank = jnp.zeros(at_pitch.shape, BF16)
    stack = []
    for k in range(3):
        stack += [(at_pitch * s[k].astype(F32)).astype(BF16) for s in split] + [blank]
    total = dot(at_span, jnp.concatenate(stack, axis=0), NT)
    wide = 4 * pitch_cells
    wall_ref[...] = -TIME_STEP * (
        total[:, 0:wide] + (total[:, wide : 2 * wide] + total[:, 2 * wide : 3 * wide])
    )

    tiles_wait(1, reply, reply_got)
    for t in range(slot_dev // LANES):
        tile = reply_got[t * per_tile * 8 : t * per_tile * 8 + 8, :]
        for k in range(t * per_tile + 1, (t + 1) * per_tile):
            tile = tile + reply_got[k * 8 : k * 8 + 8, :]
        slot_rows[:, t * LANES : (t + 1) * LANES] = tile
    metal_k = offer[1:2, :]
    used = slot_rows[2:3, :]
    temp = (slot_rows[0:1, :] + metal_k * offer[0:1, :]) / (
        slot_rows[1:2, :] * fluid_factor + metal_k * metal_factor + (1.0 - used)
    )
    metal_out_ref[...] = jnp.where(
        used > 0.5, free + BETA_METAL * metal_inv_ref[:, 0:1] * temp, old
    )

    up.wait()
    down.wait()

    @pl.when(span < n_span - 1)
    def _():
        right.wait_send()

    @pl.when(span > 0)
    def _():
        left.wait_send()

    @pl.when(span > 0)
    def _():
        right.wait_recv()

    @pl.when(span < n_span - 1)
    def _():
        left.wait_recv()


def advance_kernel(
    x_ref,
    prev_ref,
    next_ref,
    pitch_ref,
    span_ref,
    wall_ref,
    metal_ref,
    out_ref,
    metal_out_ref,
    band,
    mixed,
):
    comp = pl.program_id(0)
    part = pl.program_id(1)
    parts = pl.num_programs(1)
    chunk, span_cells, normal = x_ref.shape[1:]
    pitch_cells = wall_ref.shape[1] // 4

    @pl.when((comp == 0) & (part == 0))
    def _():
        metal_out_ref[...] = metal_ref[...]

    weight = TIME_STEP * DIFFUSION
    drift = TIME_STEP * ADVECTION * 0.5

    @pl.when((comp == 0) & (part == 0))
    def _():
        i = lax.broadcasted_iota(jnp.int32, (normal, normal), 0)
        j = lax.broadcasted_iota(jnp.int32, (normal, normal), 1)
        apart = jnp.abs(i - j)
        end = (i == 0) | (i == normal - 1)
        centre = (1.0 - 6.0 * weight) / weight
        diagonal = jnp.where(end, centre + 1.0, centre)
        one = jnp.where(apart == 1, 1.0, jnp.where(apart == 0, diagonal, 0.0)).astype(BF16)
        band[0:normal, :] = one
        band[normal : 2 * normal, :] = one

    split = pieces(x_ref[0].reshape(chunk * span_cells, normal), 2)
    mixed[...] = dot(jnp.concatenate(split, axis=1), band[...], NN)

    row = lax.broadcasted_iota(jnp.int32, (8, normal), 0)
    lane_one = lax.broadcasted_iota(jnp.int32, (span_cells, LANES), 1)
    before = jnp.where(part == 0, pitch_ref[0, 0], prev_ref[0, 0])
    after = jnp.where(part == parts - 1, pitch_ref[1, 0], next_ref[0, 0])
    for p in range(chunk):
        here = x_ref[0, p]
        prev = before if p == 0 else x_ref[0, p - 1]
        post = after if p == chunk - 1 else x_ref[0, p + 1]
        span_prev = pltpu.roll(here, 1, 0)
        first = jnp.where(row == 0, span_ref[0, 0, p : p + 1, :], span_prev[0:8])
        span_prev = jnp.concatenate([first, span_prev[8:]], axis=0)
        span_next = pltpu.roll(here, span_cells - 1, 0)
        last = jnp.where(row == 7, span_ref[1, 0, p : p + 1, :], span_next[span_cells - 8 :])
        span_next = jnp.concatenate([span_next[: span_cells - 8], last], axis=0)
        near = mixed[p * span_cells : (p + 1) * span_cells, :]
        value = (
            (weight - drift) * post
            + (weight + drift) * prev
            + weight * ((span_prev + span_next) + near)
        )
        column = comp * pitch_cells + part * chunk + p
        source = pltpu.roll(wall_ref[...], lax.rem(LANES - column, LANES), 1)
        out_ref[0, p, :, 0:LANES] = value[:, 0:LANES] + jnp.where(lane_one == 0, source, 0.0)
        out_ref[0, p, :, LANES:normal] = value[:, LANES:normal]


def vmem():
    return pl.BlockSpec(memory_space=pltpu.VMEM)


def smem():
    return pl.BlockSpec(memory_space=pltpu.SMEM)


def local(
    n_pitch,
    n_span,
    flow_state,
    wall_inverse,
    metal_inverse,
    metal_state,
    metal_conduct,
    face_coef,
    owner_map,
    face_cell,
    sample_col,
    sample_low,
):
    devices = n_pitch * n_span
    comps, pitch_cells, span_cells, normal = flow_state.shape
    slot_dev = metal_state.shape[1]
    per_peer = slot_dev // devices
    faces = owner_map.shape[0]
    any_space = pl.BlockSpec(memory_space=pl.ANY)

    wall, metal_new, pitch_halo, span_halo = pl.pallas_call(
        functools.partial(sample_kernel, n_pitch, n_span, per_peer, span_cells),
        out_shape=(
            jax.ShapeDtypeStruct((span_cells, 4 * pitch_cells), F32),
            jax.ShapeDtypeStruct(metal_state.shape, F32),
            jax.ShapeDtypeStruct((2, comps, span_cells, normal), F32),
            jax.ShapeDtypeStruct((2, comps, pitch_cells, normal), F32),
        ),
        in_specs=[smem()] * 4 + [any_space] + [vmem()] * 8,
        out_specs=[vmem()] * 4,
        scratch_shapes=[
            pltpu.VMEM((comps * 2 * pitch_cells * span_cells, LANES), F32),
            pltpu.VMEM((faces * 8, LANES), F32),
            pltpu.VMEM((LANES, LANES), F32),
            pltpu.VMEM((8, faces), F32),
            pltpu.VMEM((2, comps, pitch_cells, normal), F32),
            pltpu.VMEM((8, slot_dev), F32),
            pltpu.VMEM((devices * 8, LANES), F32),
            pltpu.VMEM((devices * 8, LANES), F32),
            pltpu.VMEM((devices * 8, LANES), F32),
            pltpu.VMEM((8, slot_dev), F32),
            pltpu.SemaphoreType.DMA((comps, 2)),
            pltpu.SemaphoreType.DMA((2,)),
            pltpu.SemaphoreType.DMA((2,)),
            pltpu.SemaphoreType.DMA((4,)),
            pltpu.SemaphoreType.DMA((4,)),
        ],
        compiler_params=pltpu.CompilerParams(
            collective_id=0, has_side_effects=True, vmem_limit_bytes=VMEM_LIMIT
        ),
        name="sample_faces",
    )(
        sample_col,
        sample_low,
        wall_inverse,
        metal_inverse,
        flow_state.reshape(comps, pitch_cells * span_cells, normal),
        sample_low.reshape(faces // LANES, LANES),
        owner_map.reshape(1, faces),
        face_cell.reshape(1, faces),
        face_coef,
        wall_inverse,
        metal_inverse,
        metal_state,
        metal_conduct.reshape(1, slot_dev),
    )

    chunk = pitch_cells // 2
    new_state, metal_out = pl.pallas_call(
        advance_kernel,
        grid=(comps, 2),
        out_shape=(
            jax.ShapeDtypeStruct(flow_state.shape, F32),
            jax.ShapeDtypeStruct(metal_state.shape, F32),
        ),
        in_specs=[
            pl.BlockSpec((1, chunk, span_cells, normal), lambda c, i: (c, i, 0, 0)),
            pl.BlockSpec(
                (1, 1, span_cells, normal),
                lambda c, i: (c, lax.rem(i * chunk + pitch_cells - 1, pitch_cells), 0, 0),
            ),
            pl.BlockSpec(
                (1, 1, span_cells, normal),
                lambda c, i: (c, lax.rem((i + 1) * chunk, pitch_cells), 0, 0),
            ),
            pl.BlockSpec((2, 1, span_cells, normal), lambda c, i: (0, c, 0, 0)),
            pl.BlockSpec((2, 1, chunk, normal), lambda c, i: (0, c, i, 0)),
            vmem(),
            vmem(),
        ],
        out_specs=[
            pl.BlockSpec((1, chunk, span_cells, normal), lambda c, i: (c, i, 0, 0)),
            pl.BlockSpec(metal_state.shape, lambda c, i: (0, 0)),
        ],
        scratch_shapes=[
            pltpu.VMEM((2 * normal, normal), BF16),
            pltpu.VMEM((chunk * span_cells, normal), F32),
        ],
        compiler_params=pltpu.CompilerParams(vmem_limit_bytes=VMEM_LIMIT),
        name="advance",
    )(
        flow_state,
        flow_state,
        flow_state,
        pitch_halo,
        span_halo,
        wall,
        metal_new,
    )
    return (new_state, metal_out)


def solution(mesh):
    return jax.shard_map(
        functools.partial(local, mesh.shape["pitch"], mesh.shape["span"]),
        mesh=mesh,
        in_specs=(
            P(None, "pitch", "span", None),
            P(),
            P(),
            P(None, ("pitch", "span")),
            P(("pitch", "span")),
            P(None, ("pitch", "span")),
            P(("pitch", "span"), None),
            P(("pitch", "span")),
            P(("pitch", "span")),
            P(("pitch", "span")),
        ),
        out_specs=(P(None, "pitch", "span", None), P(None, ("pitch", "span"))),
        check_vma=False,
    )
```
